32 devices in a mesh: dp: 8 (over z, y), mp: 4 (over x, core).
Axes of the slice: x: 2, y: 2, z: 4, core: 2. Of those that a mesh axis runs over, the one named last changes fastest.
Arguments:
- embedded: bfloat16 [640, 32, 768], P('mp', 'dp'), may hold values from -6 to 6
- cotangent: bfloat16 [640, 32, 768], P('mp', 'dp'), may hold values from -6 to 6
- lengths: int32 [32], P('dp'), may hold values from 1 to 512, as said below
- prompt: float32 [100, 768], P(None, 'dp'), may hold values from -6 to 6
- gain_one: float32 [768], replicated, may hold values from 0.5 to 1.5
- gain_two: float32 [768], replicated, may hold values from 0.5 to 1.5
- w_query: bfloat16 [768, 768], P(None, 'mp'), may hold values from -0.0546875 to 0.0546875
- w_key: bfloat16 [768, 768], P(None, 'mp'), may hold values from -0.21875 to 0.21875
- w_value: bfloat16 [768, 768], P(None, 'mp'), may hold values from -0.21875 to 0.21875
- w_output: bfloat16 [768, 768], P('mp'), may hold values from -0.625 to 0.625
- w_inner: bfloat16 [768, 3072], P(None, 'mp'), may hold values from -0.21875 to 0.21875
- w_outer: bfloat16 [3072, 768], P('mp'), may hold values from -0.15625 to 0.15625
- bias_table: float32 [32, 12], P(None, 'mp'), may hold values from -4 to 4
- left_stat: float32 [100, 100], replicated, as said below
- right_stat: float32 [768, 768], P('dp'), as said below
- left_root: float32 [100, 100], replicated, as said below
- right_root: float32 [768, 768], P('dp'), as said below
Outputs:
- layer_out: bfloat16 [640, 32, 768], P('mp', 'dp')
- embed_grad: float32 [640, 32, 768], P('mp', 'dp')
- prompt_grad: float32 [100, 768], P('mp')
- new_left: float32 [100, 100], replicated
- new_right: float32 [768, 768], P('dp')
- new_prompt: float32 [100, 768], P(None, 'dp')
The draws below stay inside these ranges and needn't reach their ends.
Inputs may be any that keep to these rules, and one draw needn't show every extreme that they name: `lengths`: in each group of 4 sequences on one index of dp, one sequence drawn from the seed has text length 640 - 640 // 4 - 99 or more; in one such group, drawn from the seed, it is exactly 512. `left_stat`: symmetric. `right_stat`: symmetric. `left_root`: symmetric. `right_root`: symmetric.
All inputs are finite; a program needn't handle non-finite values.
Results may differ from the reference program's by a relative error of at most 0.019.
Values may be sent and summed in bfloat16 or wider, within the bound.
No kernel may reach another device: no remote copies, remote signals or barrier semaphores. Data moves between devices by JAX's collectives and lax.ppermute only.
A program may use at most 384 MiB of HBM per device.

```python
import jax
import jax.numpy as jnp
from jax import lax

D = 768
HEADS = 12
HD = 64
FF = 3072
NB = 32
P_SIZE = 100
TEXT_MAX = 512
BLEN = 640
SG = 4
SEQS = 32
N_MP = 4


def symmetric(key, order, diagonal_lo, diagonal_hi, spread):
    key_diag, key_rest = jax.random.split(key)
    diagonal = jax.random.uniform(key_diag, (order,), jnp.float32, diagonal_lo, diagonal_hi)
    gauss_draw = jax.random.normal(key_rest, (order, order), jnp.float32)
    mirror = (gauss_draw + jnp.transpose(gauss_draw)) * (spread * 0.7071)
    places = jnp.arange(order)
    return jnp.where(places[:, None] == places[None, :], diagonal[:, None], mirror)


def draw_lengths(key, part):
    key = jax.random.fold_in(key, 11)
    key_base, key_shift, key_pick, key_reach, key_group = jax.random.split(key, 5)
    mantissa = jax.random.randint(key_base, (SEQS,), 1, 33)
    exponent = jax.random.randint(key_shift, (SEQS,), 0, 5)
    length = jnp.minimum(jnp.left_shift(mantissa, exponent), TEXT_MAX)
    reach = BLEN - BLEN // N_MP - P_SIZE + 1
    far_length = jax.random.randint(key_reach, (SEQS,), reach, TEXT_MAX + 1)
    chosen = jax.random.randint(key_pick, (SEQS // SG,), 0, SG)
    top_group = jax.random.randint(key_group, (), 0, SEQS // SG)
    member = jnp.arange(SEQS, dtype=jnp.int32)
    longest = member % SG == jnp.repeat(chosen, SG)
    in_top = member // SG == top_group
    far_length = jnp.where(in_top, TEXT_MAX, far_length)
    return jnp.where(longest, far_length, length).astype(jnp.int32)


def draw_left_stat(key, part):
    key = jax.random.fold_in(key, 12)
    factor = float(D * SEQS)
    return symmetric(key, P_SIZE, factor, 4.0 * factor, 0.05 * factor)


def draw_right_stat(key, part):
    key = jax.random.fold_in(key, 13)
    factor = float(P_SIZE * SEQS)
    return symmetric(key, D, factor, 4.0 * factor, 0.05 * factor)


def draw_left_root(key, part):
    key = jax.random.fold_in(key, 14)
    factor = float(SEQS) ** (-0.25)
    return symmetric(key, P_SIZE, factor, 2.0 * factor, 0.04 * factor)


def draw_right_root(key, part):
    key = jax.random.fold_in(key, 15)
    factor = float(SEQS) ** (-0.25)
    return symmetric(key, D, factor, 2.0 * factor, 0.4 * factor / float(D) ** 0.5)


def level_of(stream_key, shape, cuts, smallest, high):
    def one(dim, shards_of):
        heights = jax.random.uniform(jax.random.fold_in(jax.random.fold_in(stream_key, 6), dim), (shards_of,), jnp.float32, smallest / len(cuts), high / len(cuts))
        return jnp.repeat(jnp.exp(heights), shape[dim] // shards_of).reshape((-1,) + (1,) * (len(shape) - dim - 1))

    level = one(*cuts[0])
    for cut in cuts[1:]:
        level = level * one(*cut)
    return level


def centred(key, dims, scale, bound, cuts=(), held_as=jnp.bfloat16):
    loudness = level_of(key, dims, cuts, -0.22, 0.18) if cuts else 1.0
    array = jax.random.normal(key, dims, jnp.float32) * scale * loudness
    return jnp.minimum(jnp.maximum(array, -bound), bound).astype(held_as)


def setup_inputs(seed: int = 0) -> dict:
    splits = jax.random.split(jax.random.key(seed), 18)
    return {
        "embedded": centred(splits[0], (BLEN, SEQS, D), 1.0, 6.0, ((0, 4), (1, 8))),
        "cotangent": centred(splits[1], (BLEN, SEQS, D), 1.0, 6.0, ((0, 4), (1, 8))),
        "lengths": draw_lengths(jax.random.fold_in(splits[17], 71), 0),
        "prompt": centred(splits[3], (P_SIZE, D), 1.0, 6.0, ((1, 8),), jnp.float32),
        "gain_one": jnp.clip(1.0 + 0.1 * jax.random.normal(splits[4], (D,), jnp.float32), 0.5, 1.5),
        "gain_two": jnp.clip(1.0 + 0.1 * jax.random.normal(splits[5], (D,), jnp.float32), 0.5, 1.5),
        "w_query": centred(splits[6], (D, D), (D * HD // 4) ** -0.5, 0.0546875, ((1, 4),)),
        "w_key": centred(splits[7], (D, D), D ** -0.5, 0.21875, ((1, 4),)),
        "w_value": centred(splits[8], (D, D), D ** -0.5, 0.21875, ((1, 4),)),
        "w_output": centred(splits[9], (D, D), (D // 8) ** -0.5, 0.625, ((0, 4),)),
        "w_inner": centred(splits[10], (D, FF), D ** -0.5, 0.21875, ((1, 4),)),
        "w_outer": centred(splits[11], (FF, D), (FF // 2) ** -0.5, 0.15625, ((0, 4),)),
        "bias_table": centred(splits[12], (NB, HEADS), 1.0, 4.0, ((1, 4),), jnp.float32),
        "left_stat": draw_left_stat(jax.random.fold_in(splits[17], 71), 0),
        "right_stat": draw_right_stat(jax.random.fold_in(splits[17], 71), 0),
        "left_root": draw_left_root(jax.random.fold_in(splits[17], 71), 0),
        "right_root": draw_right_root(jax.random.fold_in(splits[17], 71), 0),
    }


PRECISE = lax.Precision.HIGHEST
EPSILON = 1e-06
DECAY_RATE = 0.5
STEP_RATE = 0.5
NEG_LARGE = -1000000000.0
THRESHOLDS = (12, 16, 23, 32, 46, 64, 91)

@jax.custom_vjp
def low(v):
    return lax.optimization_barrier(v.astype(jnp.bfloat16)).astype(jnp.float32)

@jax.custom_vjp
def low_back(v):
    return v

def low_keep(v):
    return (low(v), None)

def low_pass(kept, grad):
    return (grad,)

def back_keep(v):
    return (v, None)

def back_low(kept, grad):
    return (low(grad),)
low.defvjp(low_keep, low_pass)
low_back.defvjp(back_keep, back_low)

def rel_buckets(seq_length):
    position = jnp.arange(seq_length, dtype=jnp.int32)
    relative = position[None, :] - position[:, None]
    distance = jnp.abs(relative)
    beyond = jnp.zeros_like(distance)
    for boundary in THRESHOLDS:
        beyond = beyond + (distance >= boundary).astype(jnp.int32)
    bucket_ids = jnp.where(distance < 8, distance, 8 + beyond)
    return bucket_ids + 16 * (relative > 0).astype(jnp.int32)

def rms_norm(entries, gain):
    return entries * lax.rsqrt(lax.optimization_barrier(jnp.mean(entries * entries, axis=-1, keepdims=True)) + EPSILON) * gain

def reference(embedded, cotangent, lengths, prompt, gain_one, gain_two, w_query, w_key, w_value, w_output, w_inner, w_outer, bias_table, left_stat, right_stat, left_root, right_root):
    buckets = rel_buckets(BLEN)
    score_bias = jnp.take(jnp.transpose(bias_table).astype(jnp.float32), buckets, axis=1)
    position = jnp.arange(BLEN, dtype=jnp.int32)
    weight_query = w_query.astype(jnp.float32)
    weight_key = w_key.astype(jnp.float32)
    weight_value = w_value.astype(jnp.float32)
    weight_output = w_output.astype(jnp.float32)
    weight_inner = w_inner.astype(jnp.float32)
    weight_outer = w_outer.astype(jnp.float32)

    def layer(prompt_in, text_in, live_keys):
        layer_input = jnp.concatenate([prompt_in, text_in[P_SIZE:]], axis=0)
        normed = low(rms_norm(layer_input, gain_one))

        def project(weight):
            return low(low_back(jnp.dot(normed, weight, precision=PRECISE))).reshape(BLEN, HEADS, HD)
        queries = project(weight_query)
        keys_head = project(weight_key)
        values_head = project(weight_value)
        scores = low_back(jnp.einsum('qhd,khd->hqk', queries, keys_head, precision=PRECISE) + score_bias)
        scores = jnp.where(live_keys[None, None, :], scores, NEG_LARGE)
        softmax_out = jax.nn.softmax(scores, axis=-1)
        mixed_heads = jnp.einsum('hqk,khd->qhd', low(softmax_out), values_head, precision=PRECISE).reshape(BLEN, D)
        mixed_heads = low(low_back(mixed_heads))
        attended = low_back(jnp.dot(mixed_heads, weight_output, precision=PRECISE))
        middle = layer_input + attended
        normed_two = low(rms_norm(middle, gain_two))
        inner_act = low_back(jnp.dot(normed_two, weight_inner, precision=PRECISE))
        hidden = low(jax.nn.gelu(inner_act, approximate=True))
        outer_act = low_back(jnp.dot(hidden, weight_outer, precision=PRECISE))
        return middle + outer_act

    def one_sequence(summed, sequence):
        text_rows = lax.dynamic_index_in_dim(embedded, sequence, 1, keepdims=False).astype(jnp.float32)
        back_rows = lax.dynamic_index_in_dim(cotangent, sequence, 1, keepdims=False).astype(jnp.float32)
        live_keys = position < P_SIZE + lengths[sequence]
        result, pullback = jax.vjp(lambda prompt_in, text_in: layer(prompt_in, text_in, live_keys), prompt, text_rows)
        prompt_part, text_part = pullback(back_rows * live_keys[:, None].astype(jnp.float32))
        return (summed + prompt_part, (result.astype(jnp.bfloat16), text_part))
    gradient, (outputs, text_grads) = lax.scan(one_sequence, jnp.zeros((P_SIZE, D), jnp.float32), jnp.arange(SEQS, dtype=jnp.int32))
    layer_out = jnp.transpose(outputs, (1, 0, 2))
    embed_grad = jnp.transpose(text_grads, (1, 0, 2))
    new_left = DECAY_RATE * left_stat + (1.0 - DECAY_RATE) * jnp.dot(gradient, jnp.transpose(gradient), precision=PRECISE)
    new_right = DECAY_RATE * right_stat + (1.0 - DECAY_RATE) * jnp.dot(jnp.transpose(gradient), gradient, precision=PRECISE)
    update_step = jnp.dot(jnp.dot(left_root, gradient, precision=PRECISE), right_root, precision=PRECISE)
    new_prompt = prompt - STEP_RATE * update_step
    return (layer_out, embed_grad, gradient, new_left, new_right, new_prompt)
```

```python
import functools
import math

import jax
import jax.numpy as jnp
from jax import lax
from jax.experimental import pallas as pl
from jax.experimental.pallas import tpu as pltpu
from jax.sharding import PartitionSpec as P

EPSILON = 1e-06
DECAY_RATE = 0.5
STEP_RATE = 0.5
NEG_LARGE = -1000000000.0
THRESHOLDS = (12, 16, 23, 32, 46, 64, 91)
F32 = jnp.float32
BF16 = jnp.bfloat16
TILE = 128
TABLE_ROWS = 16
GELU_RATE = math.sqrt(2.0 / math.pi)
GELU_CUBE = 0.044715
VMEM_BYTES = 14 * 1024 * 1024
COST_SCALE = 4
FRONT_COST = 1000000000
NN = ((1,), (0,))
NT = ((1,), (1,))
TN = ((0,), (0,))


def dot(left, right, dims=NN):
    return lax.dot_general(left, right, (dims, ((), ())), preferred_element_type=F32)


def iota(dims, axis):
    return lax.broadcasted_iota(jnp.int32, dims, axis)


def taker(refs):
    refs = list(refs)
    return lambda n: [refs.pop(0) for _ in range(n)]


def mp_index():
    return lax.axis_index("mp")


def quarter_index():
    return lax.rem(lax.axis_index("dp"), 4)


def place_rows(blocks, target, shard_rows, skips=(0, 0, 0, 0)):
    for d, (block, skipped) in enumerate(zip(blocks, skips)):
        start = pl.multiple_of((mp_index() ^ d) * shard_rows, 32)
        target[pl.ds(start, shard_rows), :] = block[skipped : skipped + shard_rows, :]


def take_rows(source, blocks, shard_rows):
    for d, block in enumerate(blocks):
        start = pl.multiple_of((mp_index() ^ d) * shard_rows, 32)
        block[...] = source[pl.ds(start, shard_rows), :].astype(block.dtype)


def row_tiles(rows, height=32):
    return [slice(r, r + height) for r in range(0, rows, height)]


def peak_of(value):
    return jnp.max(value.reshape(value.shape[0] // 8, 8, value.shape[1]), axis=0)


def interleave(first, second):
    longest = max(len(first), len(second))
    for n in range(longest):
        for steps in (first, second):
            for at in range(n * len(steps) // longest, (n + 1) * len(steps) // longest):
                steps[at]()


def norm_scale(value):
    return lax.rsqrt(jnp.mean(value * value, axis=-1, keepdims=True) + EPSILON)


def norm_back(value, gain, grad):
    inverse = norm_scale(value)
    scaled = grad * gain
    mean = jnp.mean(value * scaled, axis=-1, keepdims=True)
    return scaled * inverse - value * (mean * inverse * inverse * inverse)


EARLY = ((0, 0), (0, 1), (1, 0), (2, 1))
LATE = (((1, 1), (3, 1)), ((2, 0), (3, 0)))


def place_eighths(piece, first_row, places, target):
    eighth = target.shape[0] // 8
    for n, (relative, half) in enumerate(places):
        start = pl.multiple_of(((quarter_index() ^ relative) * 2 + half) * eighth, 32)
        row = first_row + n * eighth
        target[pl.ds(start, eighth), :] = piece[row : row + eighth, :]


def join_pack(pieces, target):
    early, *late = pieces
    place_eighths(early, 0, EARLY, target)
    for piece, places in zip(late, LATE):
        place_eighths(piece, 0, places, target)


def bucket_onehot():
    relative = 2 * TILE - iota((8, 4 * TILE), 1)
    distance = jnp.abs(relative)
    bucket = jnp.minimum(distance, 8)
    for boundary in THRESHOLDS:
        bucket = bucket + (distance >= boundary).astype(jnp.int32)
    bucket = bucket + 16 * (relative > 0).astype(jnp.int32)
    return (bucket[0:1] == iota((TILE, 4 * TILE), 0)).astype(F32).astype(BF16)


def spare_queries(rows):
    tiles = rows // TILE
    row_at, tile_at = iota((64, rows), 0), iota((64, rows), 1) // TILE
    here = (row_at == 1 + tile_at) | (row_at == 1 + tiles + tile_at)
    return jnp.where((row_at == 0) | here, 1.0, 0.0).astype(BF16)


def spare_keys(rows, live, table, heads, h):
    tiles = rows // TILE
    row_at, key_at = iota((TABLE_ROWS, rows), 0), iota((TABLE_ROWS, rows), 1)
    spare = jnp.where((row_at == 0) & (key_at >= live), NEG_LARGE, 0.0)
    for part in range(2):
        ahead = key_at // TILE - (row_at - (1 + part * tiles))
        inside = (row_at > part * tiles) & (row_at <= (part + 1) * tiles)
        at = part * heads + h
        right = jnp.where(inside & (ahead >= 2), 1.0, 0.0)
        left = jnp.where(inside & (ahead <= -2), 1.0, 0.0)
        spare = spare + right * table[at : at + 1, 31:32] + left * table[at : at + 1, 15:16]
    return spare.astype(BF16)


def filler_rows(rows):
    return jnp.zeros((64 - TABLE_ROWS, rows), BF16)


def split_kernel(cfg, source, *outs):
    for start, out in zip(cfg, outs):
        out[...] = source[start : start + out.shape[0], :]


def join_kernel(near, far, near_next, far_next, first, second, early):
    size = near.shape[0]
    outs = ((first, (far, far_next)), (second, (near, near_next)))
    outs += ((early, (near, far, near_next, far_next)),)
    for out, pieces in outs:
        for n, piece in enumerate(pieces):
            out[n * size : (n + 1) * size, :] = piece[...]


def live_kernel(cfg, lengths_ref, live_ref):
    (prompt_rows,) = cfg
    live_ref[...] = jnp.full(live_ref.shape, prompt_rows + lengths_ref[mp_index()], jnp.int32)


def gather_kernel(*refs):
    *pieces, out, top, bottom = refs
    join_pack(pieces, out)
    half = top.shape[0]
    top[...] = out[0:half, :]
    bottom[...] = out[half : 2 * half, :]


def stack_kernel(top, bottom, out):
    half = top.shape[0]
    out[0:half, :] = top[...]
    out[half : 2 * half, :] = bottom[...]


def first_kernel(cfg, *refs):
    heads, buckets, shard_rows = cfg
    take = taker(refs)
    weights = take(4)
    w_in, w_out, text_in, table_in, share, *text = take(8)
    (packed,) = take(1)
    text_ref, table_ref, by_seq, sems = take(4)
    inner = weights[0].shape[0]
    size = share.shape[0] - inner
    feed_at = 4 * inner

    def copies_of(at):
        feed = (w_in, w_out)[at // 2].at[pl.ds(at % 2 * size, size)]
        return [
            pltpu.make_async_copy(weights[at], share.at[pl.ds(0, inner)], sems.at[0]),
            pltpu.make_async_copy(feed, share.at[pl.ds(inner, size)], sems.at[1]),
        ]

    own = [
        pltpu.make_async_copy(text_in, text_ref, sems.at[2]),
        pltpu.make_async_copy(table_in, table_ref, sems.at[3]),
    ]
    whole = []
    for n, weight in enumerate(weights):
        place = packed.at[pl.ds(n * inner, inner)]
        whole.append(pltpu.make_async_copy(weight, place, sems.at[4 + n]))
    for n, weight in enumerate((w_in, w_out)):
        rows = weight.shape[0]
        place = packed.at[pl.ds(feed_at + n * rows, rows)]
        whole.append(pltpu.make_async_copy(weight, place, sems.at[8 + n]))
    for copy in own:
        copy.start()
    for at in range(4):

        @pl.when(quarter_index() == at)
        def _(at=at):
            for copy in copies_of(at):
                copy.start()

    for copy in whole:
        copy.start()
    for copy in own:
        copy.wait()
    for s in range(4):
        by_seq[s] = text_ref[:, s, :]
    wide = jnp.concatenate([table_ref[...], jnp.zeros((heads, TILE - buckets), F32)], axis=1)
    high = wide.astype(BF16)
    low = (wide - high.astype(F32)).astype(BF16)
    rest = jnp.zeros((TABLE_ROWS - 2 * heads, TILE), F32)
    table = jnp.concatenate([high.astype(F32), low.astype(F32), rest], axis=0).astype(BF16)
    for d in range(4):
        out, start = text[min(d, 2)], (shard_rows + TABLE_ROWS) * (d == 3)
        end = start + shard_rows
        out[start:end, :] = by_seq[mp_index() ^ d]
        out[end : end + TABLE_ROWS, :] = jnp.zeros((TABLE_ROWS, text_ref.shape[2]), BF16)
        out[end : end + TABLE_ROWS, 0:TILE] = table
    for copy in [*copies_of(0), *whole]:
        copy.wait()


def cot_kernel(cot_ref, mine, near, far, by_seq):
    for s in range(4):
        by_seq[s] = cot_ref[:, s, :]
    mine[...] = by_seq[mp_index()]
    near[...] = by_seq[mp_index() ^ 1]
    size = mine.shape[0]
    for n in range(2):
        far[n * size : (n + 1) * size, :] = by_seq[mp_index() ^ (2 + n)]


def merge_kernel(*refs):
    *blocks, out, by_seq = refs
    for d, block in enumerate(blocks):
        by_seq[mp_index() ^ d] = block[...]
    for s in range(len(blocks)):
        out[:, s, :] = by_seq[s].astype(out.dtype)


def sum_kernel(*refs):
    *parts, out = refs
    values = [part[...].astype(F32) for part in parts]
    while len(values) > 1:
        values = [values[n] + values[n + 1] for n in range(0, len(values), 2)]
    out[...] = values[0].astype(BF16)


def append_kernel(mine, other, near, across, diagonal, total, *outs):
    total[...] = (mine[...].astype(F32) + other[...].astype(F32)).astype(BF16)
    half = diagonal.shape[0] // 2
    pieces = (near[...], across[...], diagonal[0:half, :], diagonal[half : 2 * half, :])
    for n, (piece, out) in enumerate(zip(pieces, outs)):
        size = piece.shape[0]
        out[0:size, :] = piece
        if n < 2:
            out[size : out.shape[0], :] = total[...]


def narrow_kernel(source, out):
    out[...] = jnp.zeros_like(out)
    out[:, 0 : source.shape[1]] = source[...].astype(BF16)


def natural_kernel(cfg, *refs):
    axis_step, count = cfg
    *pieces, out = refs
    index = lax.rem(lax.axis_index("dp") // axis_step, count)
    size = pieces[0].shape[0]
    for s in range(count):
        value = pieces[s][...]
        for at in range(1, count):
            value = jnp.where(index == at, pieces[s ^ at][...], value)
        out[s * size : (s + 1) * size, :] = value


def run_scores(cfg, tables, refs):
    s, rows, heads, size, live, onehot, filler, ones, one_row = cfg
    table32, lines = tables
    qkv_ref, mixed_ref, inv_ref, exp_ref, scores = refs
    inner = heads * size
    tiles = rows // TILE
    wide = 2 * TILE
    halves = row_tiles(rows, rows // 2)
    head_data = {}

    def of_head(h):
        if h not in head_data:
            keys = qkv_ref[s, inner + h * size : inner + (h + 1) * size]
            spare = spare_keys(rows, live, table32, heads, h)
            line = lines[h : h + 1] + lines[heads + h : heads + h + 1]
            values = qkv_ref[s, 2 * inner + h * size : 2 * inner + (h + 1) * size]
            head_data[h] = (
                jnp.concatenate([keys, spare, filler], axis=0).T,
                pltpu.roll(
                    jnp.broadcast_to(line, (TILE, 4 * TILE)), 0, 1, stride=1, stride_axis=0
                ),
                jnp.concatenate([values, one_row], axis=0),
            )
        return head_data[h]

    blocks = [
        (h, start, min(wide, rows - start)) for h in range(heads) for start in range(0, rows, wide)
    ]

    def score(n):
        h, start, span = blocks[n]
        keys = of_head(h)[0]
        queries = qkv_ref[s, h * size : (h + 1) * size, start : start + span]
        queries = jnp.concatenate([queries, ones[:, start : start + span]], axis=0)

        def half(at):
            scores[n % 2, at, 0:span] = dot(keys[at, :], queries)

        return [functools.partial(half, at) for at in halves]

    def soften(n):
        h, start, span = blocks[n]
        turned = of_head(h)[1]
        steps = []
        for column in range(0, span, TILE):
            q = (start + column) // TILE
            peaks = []

            def part_of(k, part, q=q, column=column):
                at = k * TILE + part
                value = scores[n % 2, at : at + 64, column : column + TILE]
                if abs(k - q) <= 1:
                    offset = (2 - (k - q)) * TILE
                    value = value + turned[part : part + 64, offset : offset + TILE]
                return value

            places = [(k, part) for k in range(tiles) for part in range(0, TILE, 64)]

            def peak(part_of=part_of, peaks=peaks):
                value = functools.reduce(jnp.maximum, [peak_of(part_of(*p)) for p in places])
                peaks.append(jnp.max(value, axis=0, keepdims=True))

            def power(some, q=q, part_of=part_of, peaks=peaks):
                for k, part in some:
                    at = slice(k * TILE + part, k * TILE + part + 64)
                    value = jnp.exp(part_of(k, part) - peaks[0])
                    exp_ref[s, h, at, q * TILE : (q + 1) * TILE] = value.astype(BF16)

            steps.append(peak)
            steps += [functools.partial(power, places[m : m + 5]) for m in range(0, len(places), 5)]
        return steps

    def mix(n):
        h, start, span = blocks[n]
        columns = slice(start, start + span)
        mixed = dot(of_head(h)[2], exp_ref[s, h, :, columns])
        inverse = 1.0 / mixed[size : size + 1]
        inv_ref[s, h : h + 1, columns] = inverse
        mixed_ref[s, h * size : (h + 1) * size, columns] = (mixed[0:size] * inverse).astype(BF16)

    for step in score(0):
        step()
    for n in range(len(blocks)):
        beside = score(n + 1) if n + 1 < len(blocks) else []
        if n > 0:
            beside = beside + [functools.partial(mix, n - 1)]
        interleave(beside, soften(n))
    mix(len(blocks) - 1)


def attend_kernel(cfg, *refs):
    first, last, shards, rows, width, heads, size, shard_rows, prompt_rows, table_at = cfg
    inner = heads * size
    take = taker(refs)
    (live_ref,) = take(1)
    if first:
        blocks = take(4)
        prompt_ref, gain_ref = take(2)
        tables = blocks
    else:
        tables = take(shards)
        turned_ref, start_ref, gain_ref = take(3)
    packs = take(shards)
    (acc_ref,) = take(1)
    if first:
        x_ref, turned_ref = take(2)
    if last:
        (normed_two_ref,) = take(1)
    qkv_ref, mixed_ref, inv_ref, exp_ref = take(4)
    (scores,) = take(1)
    if first:
        (normed_ref,) = take(1)
        place_rows(blocks, x_ref, shard_rows)
        top = -(-prompt_rows // 16) * 16
        head = prompt_ref[...].T[0:top]
        at = iota((top, width), 0)
        x_ref[0:top, :] = jnp.where(at < prompt_rows, head, x_ref[0:top, :])
        for at in row_tiles(rows):
            x = x_ref[at, :].astype(F32)
            normed_ref[at, :] = (x * norm_scale(x) * gain_ref[...]).astype(BF16)
        turned_ref[...] = normed_ref[...].T

    tiles = rows // TILE
    live = live_ref[0:1, 0:1]
    filler = filler_rows(rows)
    ones = spare_queries(rows)
    onehot = bucket_onehot()
    one_row = jnp.where(iota((TABLE_ROWS, rows), 0) == 0, 1.0, 0.0).astype(BF16)

    for s in range(shards):
        pack = packs[s]
        qkv_ref[s] = dot(pack[0 : 3 * inner], turned_ref[...]).astype(BF16)
        table = tables[s][table_at : table_at + TABLE_ROWS, 0:TILE]
        lines = dot(table, onehot)
        table32 = table.astype(F32)
        run_scores(
            (s, rows, heads, size, live, onehot, filler, ones, one_row),
            (table32, lines),
            (qkv_ref, mixed_ref, inv_ref, exp_ref, scores),
        )
        part = dot(mixed_ref[s].T, pack[3 * inner : 4 * inner])
        if s == 0:
            acc_ref[...] = part + (x_ref[...].astype(F32) if first else start_ref[...])
        else:
            acc_ref[...] += part

    if last:
        for at in row_tiles(rows):
            middle = acc_ref[at, :]
            normed_two_ref[at, :] = (middle * norm_scale(middle) * gain_ref[...]).astype(BF16)


def feed_kernel(cfg, *refs):
    first, last, shards, rows, width, shard_rows, prompt_rows, feed_at = cfg
    take = taker(refs)
    (normed_ref,) = take(1)
    if first:
        start_ref, live_ref = take(2)
        blocks = take(4)
    else:
        low_ref, start_ref, back_in = take(3)
    if last:
        middle_ref, gain_ref = take(2)
    packs = [take(1 if first else 3) for _ in range(shards)]
    if first:
        (low_ref,) = take(1)
    if last:
        outs = take(4)
        (back_middle_ref,) = take(1)
    else:
        outer_ref, back_ref = take(2)
    act_ref, grad_ref, hidden_ref, slope_ref = take(4)
    if last:
        outer_ref, back_ref = take(2)
    if not first:
        (joined,) = take(1)

    if first:
        place_rows(blocks, low_ref, shard_rows)
        live = live_ref[0:1, 0:1]
        for at in row_tiles(rows):
            here = iota((32, width), 0) + at.start < live
            low_ref[at, :] = jnp.where(here, low_ref[at, :], jnp.zeros((32, width), BF16))

    for s in range(shards):
        if first:
            (pack,) = packs[s]
            w_in = pack.at[pl.ds(feed_at, width)]
            w_out = pack.at[pl.ds(feed_at + width, width)]
        else:
            join_pack(packs[s], joined)
            w_in = joined.at[pl.ds(0, width)]
            w_out = joined.at[pl.ds(width, width)]
        act_ref[...] = dot(normed_ref[...], w_in[...])
        grad_ref[...] = dot(low_ref[...], w_out[...], NT)
        for at in row_tiles(rows):
            for column in range(0, act_ref.shape[1], 2 * TILE):
                columns = slice(column, column + 2 * TILE)
                act = act_ref[at, columns]
                square = act * act
                curve = jnp.tanh(act * (GELU_RATE + (GELU_RATE * GELU_CUBE) * square))
                half = 0.5 + 0.5 * curve
                hidden_ref[at, columns] = (act * half).astype(BF16)
                slope = half + (act * (0.5 - 0.5 * curve * curve)) * (
                    GELU_RATE + (3.0 * GELU_RATE * GELU_CUBE) * square
                )
                slope_ref[at, columns] = (grad_ref[at, columns] * slope).astype(BF16)
        outer_from = start_ref if s == 0 else outer_ref
        outer_ref[...] = outer_from[...] + dot(hidden_ref[...], w_out[...])
        back = dot(slope_ref[...], w_in[...], NT)
        if s == 0 and first:
            back_ref[...] = back
        else:
            back_from = back_in if s == 0 else back_ref
            back_ref[...] = back_from[...] + back

    if last:
        take_rows(outer_ref, outs, shard_rows)
        for at in row_tiles(rows):
            back = norm_back(middle_ref[at, :], gain_ref[...], back_ref[at, :])
            back_middle_ref[at, :] = (low_ref[at, :].astype(F32) + back).astype(BF16)


def back_parts(row_at, filler, two_rows, grads, inverse, values, mixed):
    scaled = (grads.astype(F32) * inverse).astype(BF16)
    term = jnp.sum(scaled.astype(F32) * mixed.astype(F32), axis=0, keepdims=True)
    high = term.astype(BF16).astype(F32)
    spare = jnp.where(row_at == 0, -high, jnp.where(row_at == 1, high - term, 0.0)).astype(BF16)
    values_wide = jnp.concatenate([values, two_rows, filler], axis=0).T
    return scaled, jnp.concatenate([scaled, spare, filler], axis=0), values_wide


def spare_rows(rows):
    row_at = iota((TABLE_ROWS, rows), 0)
    return row_at, filler_rows(rows), jnp.where(row_at < 2, 1.0, 0.0).astype(BF16)


def back_top_kernel(cfg, *refs):
    rows, width, heads, size, groups, top_rows, kept_counts = cfg
    inner = heads * size
    take = taker(refs)
    back_ref, x_ref, gain_ref = take(3)
    packs = take(groups)
    kept = []
    for count in kept_counts:
        group = take(4)
        kept += [[ref.at[n] for ref in group] for n in range(count)]
    top_ref, mixed_grad_ref = take(2)
    outs = take(4)
    weights, joint, acc_ref, top_raw, left_raw, top_ds, left_ds = take(7)

    row_at, filler, two_rows = spare_rows(rows)
    for s in range(groups):
        weights[s * inner : (s + 1) * inner, :] = packs[s][3 * inner : 4 * inner]
    grads_all = dot(weights[...], back_ref[...], NT).astype(BF16)
    for s in range(groups):
        mixed_grad_ref[s] = grads_all[s * inner : (s + 1) * inner]
    places = [(s, h) for s in range(groups) for h in range(heads)]
    scaled = []
    for n, (s, h) in enumerate(places):
        qkv_ref, mixed_ref, inv_ref, exp_ref = kept[s]
        at = slice(h * size, (h + 1) * size)
        values_at = slice(2 * inner + h * size, 2 * inner + (h + 1) * size)
        scale, wide, values = back_parts(
            row_at,
            filler,
            two_rows,
            mixed_grad_ref[s, at],
            inv_ref[h : h + 1, :],
            qkv_ref[values_at],
            mixed_ref[at],
        )
        scaled.append(scale)
        top_raw[n] = dot(values[0:TILE], wide)
        left_raw[n] = dot(values[TILE:rows], wide[:, 0:TILE])
    for n, (s, h) in enumerate(places):
        exp_ref = kept[s][3]
        for column in range(0, rows, TILE):
            columns = slice(column, column + TILE)
            for row in row_tiles(TILE, 64):
                top_ds[n, row, columns] = (
                    exp_ref[h, row, columns].astype(F32) * top_raw[n, row, columns]
                ).astype(BF16)
        for row in row_tiles(rows - TILE, 64):
            below = slice(row.start + TILE, row.stop + TILE)
            left_ds[n, row, :] = (
                exp_ref[h, below, 0:TILE].astype(F32) * left_raw[n, row, :]
            ).astype(BF16)
    for n, (s, h) in enumerate(places):
        qkv_ref, mixed_ref, inv_ref, exp_ref = kept[s]
        at = slice(h * size, (h + 1) * size)
        keys_at = slice(inner + h * size, inner + (h + 1) * size)
        values_at = slice(2 * inner + h * size, 2 * inner + (h + 1) * size)
        joint[s, at] = (
            dot(qkv_ref[keys_at, 0:TILE], top_ds[n, :, 0:TILE])
            + dot(qkv_ref[keys_at, TILE:rows], left_ds[n])
        ).astype(BF16)
        joint[s, keys_at] = dot(qkv_ref[at], top_ds[n], NT).astype(BF16)
        joint[s, values_at] = dot(scaled[n], exp_ref[h, 0:TILE], NT).astype(BF16)
    for s in range(groups):
        part = dot(joint[s].T, packs[s][0 : 3 * inner])
        if s == 0:
            acc_ref[...] = part
        else:
            acc_ref[...] += part
    for at in row_tiles(TILE):
        back = norm_back(x_ref[at, :].astype(F32), gain_ref[...], acc_ref[at, :])
        acc_ref[at, :] = back_ref[at, :].astype(F32) + back
    top_ref[...] = acc_ref[...].astype(BF16)
    take_rows(acc_ref, outs, top_rows)


def back_rest_kernel(cfg, *refs):
    s, last, rows, width, heads, size, shard_rows, prompt_rows = cfg
    inner = heads * size
    rest = rows - TILE
    take = taker(refs)
    pack, qkv, mixed, inv, exp, mixed_grad_ref = take(6)
    qkv_ref, mixed_ref, inv_ref, exp_ref = [ref.at[0] for ref in (qkv, mixed, inv, exp)]
    if s > 0:
        (start_ref,) = take(1)
    if last:
        back_ref, x_ref, gain_ref, top_ref = take(4)
        outs = take(4)
    else:
        (acc_ref,) = take(1)
    raw, score_grads, joint = take(3)
    if last:
        acc_ref, whole_ref = take(2)

    row_at, filler, two_rows = spare_rows(rows)
    head_data = {}

    def of_head(h):
        if h not in head_data:
            at = slice(h * size, (h + 1) * size)
            values_at = slice(2 * inner + h * size, 2 * inner + (h + 1) * size)
            head_data[h] = back_parts(
                row_at,
                filler,
                two_rows,
                mixed_grad_ref[s, at],
                inv_ref[h : h + 1, :],
                qkv_ref[values_at],
                mixed_ref[at],
            )
        return head_data[h]

    span = 2 * TILE
    blocks = [
        (h, start, min(span, rows - start)) for h in range(heads) for start in range(0, rows, span)
    ]
    halves = row_tiles(rows, rows // 2)

    def prob(n):
        h, start, size_now = blocks[n]
        _, wide, values = of_head(h)

        def half(at):
            raw[n % 2, at, 0:size_now] = dot(values[at, :], wide[:, start : start + size_now])

        return [functools.partial(half, at) for at in halves]

    def scored(n):
        h, start, size_now = blocks[n]

        def tile(row):
            for column in range(0, size_now, TILE):
                at = slice(start + column, start + column + TILE)
                score_grads[h, row, at] = (
                    exp_ref[h, row, at].astype(F32) * raw[n % 2, row, column : column + TILE]
                ).astype(BF16)

        return [functools.partial(tile, row) for row in row_tiles(rows, 64)]

    def outputs(h):
        at = slice(h * size, (h + 1) * size)
        keys_at = slice(inner + h * size, inner + (h + 1) * size)
        values_at = slice(2 * inner + h * size, 2 * inner + (h + 1) * size)

        def queries():
            joint[at] = dot(qkv_ref[keys_at], score_grads[h, :, TILE:rows]).astype(BF16)

        def keys():
            joint[keys_at] = dot(qkv_ref[at], score_grads[h, TILE:rows], NT).astype(BF16)

        def values():
            joint[values_at] = dot(of_head(h)[0], exp_ref[h, TILE:rows], NT).astype(BF16)

        return [queries, keys, values]

    for step in prob(0):
        step()
    waiting = []
    for n in range(len(blocks)):
        beside = prob(n + 1) if n + 1 < len(blocks) else []
        interleave(beside + waiting, scored(n))
        h, start, size_now = blocks[n]
        waiting = outputs(h) if start + size_now == rows else []
    for step in waiting:
        step()
    part = dot(joint[...].T, pack[0 : 3 * inner])
    acc_ref[...] = part + start_ref[...] if s > 0 else part

    if last:
        at = iota((TILE, width), 0)
        whole_ref[0:TILE, :] = jnp.where(at < prompt_rows, 0.0, top_ref[...].astype(F32))
        for at in row_tiles(rest):
            below = slice(at.start + TILE, at.stop + TILE)
            back = norm_back(x_ref[below, :].astype(F32), gain_ref[...], acc_ref[at, :])
            whole_ref[below, :] = back_ref[below, :].astype(F32) + back
        take_rows(whole_ref, outs, shard_rows)


def split_dot(left, right, dims):
    high = left.astype(BF16)
    low = (left - high.astype(F32)).astype(BF16)
    return dot(high, right, dims) + dot(low, right, dims)


def embed_kernel(cfg, *refs):
    start, count, starts = cfg
    blocks = refs[: len(starts)]
    out, by_seq, whole, sems = refs[-4:]
    for d, (block, first) in enumerate(zip(blocks, starts)):
        by_seq[mp_index() ^ d] = block[first : first + count, :]
    copies = []
    for n, at in enumerate(row_tiles(count, count // 2)):
        for s in range(len(starts)):
            whole[at, s, :] = by_seq[s, at, :].astype(F32)
        there = out.at[pl.ds(start + at.start, count // 2)]
        copies.append(pltpu.make_async_copy(whole.at[at], there, sems.at[n]))
        copies[-1].start()
    for copy in copies:
        copy.wait()


def step_kernel(cfg, *refs):
    prompt_rows, groups, starts = cfg
    take = taker(refs)
    blocks = take(groups)
    left_stat, right_stat, left_root, right_root, prompt_ref = take(5)
    block_ref, left_ref, right_ref, new_ref, gradient = take(5)
    share = gradient.shape[0] // groups
    for d, (block, first) in enumerate(zip(blocks, starts)):
        start = pl.multiple_of((mp_index() ^ d) * share, 32)
        gradient[pl.ds(start, share), :] = block[first : first + share, :]
    rows, width = gradient.shape
    live = iota((rows, width), 0) < prompt_rows
    grad = jnp.where(live, gradient[...], jnp.zeros_like(gradient))
    own = right_stat.shape[0]
    share_rows = prompt_rows // groups

    here = iota((share_rows, rows), 1) == iota((share_rows, rows), 0) + mp_index() * share_rows
    block_ref[...] = dot(here.astype(F32).astype(BF16), grad)
    gram = dot(grad, grad, NT)[0:prompt_rows, 0:prompt_rows]
    left_ref[...] = DECAY_RATE * left_stat[...] + (1.0 - DECAY_RATE) * gram
    mine = iota((width, own), 0) == iota((width, own), 1) + lax.axis_index("dp") * own
    columns = dot(grad, mine.astype(F32).astype(BF16)).astype(BF16)
    right_ref[...] = DECAY_RATE * right_stat[...] + (1.0 - DECAY_RATE) * dot(columns, grad, TN)
    side = split_dot(right_root[...], grad, NT)[:, 0:prompt_rows]
    high = side.astype(BF16)
    low = (side - high.astype(F32)).astype(BF16)
    root = left_root[...]
    root_high = root.astype(BF16)
    root_low = (root - root_high.astype(F32)).astype(BF16)
    update = dot(high, root_high, NT) + dot(high, root_low, NT) + dot(low, root_high, NT)
    new_ref[...] = prompt_ref[...] - STEP_RATE * update


def on_device(
    embedded,
    cotangent,
    lengths,
    prompt,
    gain_one,
    gain_two,
    w_query,
    w_key,
    w_value,
    w_output,
    w_inner,
    w_outer,
    bias_table,
    left_stat,
    right_stat,
    left_root,
    right_root,
):
    shard_rows, group_seqs, width = embedded.shape
    groups = lax.axis_size("mp")
    dp_size = lax.axis_size("dp")
    rows = shard_rows * groups
    prompt_rows, prompt_cols = prompt.shape
    buckets, heads = bias_table.shape
    inner = w_query.shape[1]
    size = inner // heads
    units = w_inner.shape[1]
    assert groups == 4 and group_seqs == groups and units == width and dp_size % 4 == 0
    VMEM, HBM = pltpu.VMEM, pltpu.HBM

    def hop(value, distance):
        return lax.ppermute(value, "mp", [(i, i ^ distance) for i in range(groups)])

    def hop_dp(value, distance):
        return lax.ppermute(value, "dp", [(i, i ^ distance) for i in range(dp_size)])

    def exchange(pieces):
        return [pieces[0]] + [hop(pieces[d], d) for d in range(1, groups)]

    def after(value, *others):
        return lax.optimization_barrier((value, *others))[0]

    def call(kernel, ins, outs, scratch=(), flops=0, far=0, lead=(), out_space=VMEM, far_outs=0, far_last=0):
        spaces = [HBM] * far + [VMEM] * (len(ins) - far - far_last) + [HBM] * far_last
        held = [pltpu.with_memory_space_constraint(v, space) for v, space in zip(ins, spaces)]
        made = [
            VMEM(dims, kind) if out_space is VMEM else jax.ShapeDtypeStruct(dims, kind)
            for dims, kind in outs
        ]
        out_spaces = [HBM] * far_outs + [VMEM] * (len(outs) - far_outs)
        results = pl.pallas_call(
            kernel,
            in_specs=[pl.BlockSpec(memory_space=pltpu.SMEM)] * len(lead)
            + [pl.BlockSpec(memory_space=space) for space in spaces],
            out_specs=[pl.BlockSpec(memory_space=space) for space in out_spaces],
            out_shape=made,
            input_output_aliases={len(lead) + len(ins) - 1: 0} if far_last else {},
            scratch_shapes=[
                VMEM(*each) if isinstance(each, tuple) else each for each in scratch
            ],
            compiler_params=pltpu.CompilerParams(vmem_limit_bytes=VMEM_BYTES),
            cost_estimate=pl.CostEstimate(
                flops=COST_SCALE * flops, bytes_accessed=0, transcendentals=0
            ),
        )(*lead, *held)
        return results

    low_block = lambda n: ((n, width), BF16)

    gain_first = gain_one[None, :]
    gain_second = gain_two[None, :]
    weights = [w_query.T, w_key.T, w_value.T, w_output]
    dma = pltpu.SemaphoreType.DMA

    lengthy = shard_rows + TABLE_ROWS
    feed_at = 4 * inner
    made = call(
        functools.partial(first_kernel, (heads, buckets, shard_rows)),
        [*weights, w_inner, w_outer, embedded, bias_table.T],
        [low_block(inner + units // 2)]
        + [low_block(lengthy)] * 2
        + [low_block(2 * lengthy), low_block(feed_at + 2 * units)],
        [
            (embedded.shape, BF16),
            ((heads, buckets), F32),
            ((groups, shard_rows, width), BF16),
            dma((10,)),
        ],
        far=8,
    )
    share, text_pieces, pack = made[0], made[1:4], made[4]
    share = hop(share, 2)

    (block,) = call(narrow_kernel, [after(prompt.T, pack)], [((prompt_cols, TILE), BF16)])

    def wider(block, step):
        other = hop_dp(block, step)
        dims = ((2 * block.shape[0], TILE), BF16)
        kernel = functools.partial(natural_kernel, (step, 2))
        return call(kernel, [block, other], [dims])[0]

    step = 1
    while 2 * step < dp_size:
        block = wider(block, step)
        step *= 2

    beside = hop(pack, 1)
    (live,) = call(
        functools.partial(live_kernel, (prompt_rows,)),
        [],
        [((8, TILE), jnp.int32)],
        lead=(after(lengths, pack),),
    )
    text_near = hop(after(text_pieces[1], pack), 1)
    cot_mine, cot_near, cot_far = call(
        cot_kernel,
        [after(cotangent, block)],
        [low_block(shard_rows)] * 2 + [low_block(2 * shard_rows)],
        [((groups, shard_rows, width), BF16)],
    )
    cot_near = hop(cot_near, 1)
    block = wider(block, step)
    share = after(share, block, beside, text_near, cot_near, live)
    small, large = low_block(inner // 2), low_block(units // 4)
    starts = (0, inner // 2, inner, inner + units // 4)
    attend_near, attend_far, feed_near, feed_far = call(
        functools.partial(split_kernel, starts),
        [share],
        [small, small, large, large],
    )
    text_far = hop(text_pieces[2], 2)

    def first_round(near, far):
        return near, far, hop_dp(near, 1), hop_dp(far, 2)

    def joined(pieces):
        half = pieces[0].shape[0]
        return call(join_kernel, pieces, [low_block(2 * half)] * 2 + [low_block(4 * half)])

    pack_round = first_round(attend_near, attend_far)
    feed_round = first_round(feed_near, feed_far)
    first, second, pack_early = joined(pack_round)
    pack_late = hop_dp(first, 1), hop_dp(second, 2)
    feed_first, feed_second, early = joined(feed_round)
    feed_late = hop_dp(feed_first, 1), hop_dp(feed_second, 2)
    text_far = after(text_far, first)
    (passed,) = call(
        functools.partial(split_kernel, (lengthy,)), [text_far], [low_block(lengthy)]
    )
    text = [text_pieces[0], text_near, text_far, hop(passed, 1)]

    wide_low, wide_full = ((rows, width), BF16), ((rows, width), F32)

    def kept_of(shards):
        return [
            ((shards, 3 * inner, rows), BF16),
            ((shards, inner, rows), BF16),
            ((shards, 8, rows), F32),
            ((shards, heads, rows, rows), BF16),
        ]

    def attend_call(first, last, ins, outs, table_at=shard_rows):
        shards = 1
        cfg = (first, last, shards, rows, width, heads, size, shard_rows, prompt_rows)
        cfg += (table_at,)
        return call(
            functools.partial(attend_kernel, cfg),
            [live, *ins],
            [wide_full] + outs + kept_of(shards),
            [((2, rows, 2 * TILE), F32)] + ([wide_low] if first else []),
            2 * shards * rows * (4 * inner * width + 2 * inner * rows),
        )

    part, x, normed, *kept_own = attend_call(
        True, False, [*text, block, gain_first, pack], [wide_low, ((width, rows), BF16)]
    )
    pack_round = [*pack_round[:3], after(pack_round[3], part)]
    cot_far = hop(after(cot_far, text_far), 2)
    part, *kept_beside = attend_call(
        False, False, [text[1], normed, after(part, feed_first), gain_second, beside], []
    )
    (cot_passed,) = call(
        functools.partial(split_kernel, (shard_rows,)), [cot_far], [low_block(shard_rows)]
    )
    cot = [cot_mine, cot_near, cot_far, hop(cot_passed, 1)]
    far_pack, *far_halves = call(
        gather_kernel,
        [pack_early, *(after(piece, part) for piece in pack_late)],
        [low_block(4 * inner)] + [low_block(2 * inner)] * 2,
    )
    far_halves = [hop(piece, 1) for piece in far_halves]
    (last_pack,) = call(stack_kernel, far_halves, [low_block(4 * inner)])
    part, *kept_far = attend_call(
        False,
        False,
        [text[2], normed, after(part, cot_passed), gain_second, far_pack],
        [],
    )
    middle, normed_two, *kept_last = attend_call(
        False,
        True,
        [text[3], normed, part, gain_second, last_pack],
        [wide_low],
    )

    def feed_call(first, last, shards, ins, outs):
        cfg = (first, last, shards, rows, width, shard_rows, prompt_rows, feed_at)
        scratch = [((rows, units), F32)] * 2 + [((rows, units), BF16)] * 2
        scratch += [wide_full, wide_full] if last else []
        return call(
            functools.partial(feed_kernel, cfg),
            ins,
            outs,
            scratch + ([] if first else [((2 * width, units), BF16)]),
            2 * 4 * shards * rows * width * units,
        )

    low, outer, back = feed_call(
        True,
        False,
        2,
        [normed_two, middle, live, *cot, pack, beside],
        [wide_low, wide_full, wide_full],
    )
    early_next = hop(after(early, middle), 1)
    late_next = [hop(after(piece, outer), 1) for piece in feed_late]
    outer, back = feed_call(
        False,
        False,
        1,
        [normed_two, low, outer, back, early, *feed_late],
        [wide_full, wide_full],
    )
    *layer_pieces, back_middle = feed_call(
        False,
        True,
        1,
        [normed_two, low, outer, back, middle, gain_second, early_next, *late_next],
        [low_block(shard_rows)] * groups + [wide_low],
    )

    packs = [pack, beside, far_pack, last_pack]
    kept_groups = [kept_own, kept_beside, kept_far, kept_last]
    top_rows = TILE // groups
    top_grad, mixed_grad, *top_pieces = call(
        functools.partial(
            back_top_kernel, (rows, width, heads, size, groups, top_rows, (1, 1, 1, 1))
        ),
        [back_middle, x, gain_first, *packs, *(ref for group in kept_groups for ref in group)],
        [low_block(TILE), ((groups, inner, rows), BF16)] + [low_block(top_rows)] * groups,
        [
            ((groups * inner, width), BF16),
            ((groups, 3 * inner, TILE), BF16),
            ((TILE, width), F32),
            ((groups * heads, TILE, rows), F32),
            ((groups * heads, rows - TILE, TILE), F32),
            ((groups * heads, TILE, rows), BF16),
            ((groups * heads, rows - TILE, TILE), BF16),
        ],
        2 * groups * rows * 2 * inner * width,
    )

    top_got = exchange(top_pieces)

    def rest_call(s, ins):
        last = s == groups - 1
        cfg = (s, last, rows, width, heads, size, shard_rows, prompt_rows)
        rest = ((rows - TILE, width), F32)
        scratch = [
            ((2, rows, 2 * TILE), F32),
            ((heads, rows, rows), BF16),
            ((3 * inner, rows - TILE), BF16),
        ]
        return call(
            functools.partial(back_rest_kernel, cfg),
            [packs[s], *kept_groups[s], *ins],
            [low_block(shard_rows)] * groups if last else [rest],
            scratch + ([rest, wide_full] if last else []),
            2 * rows * (3 * inner * width + 4 * inner * rows),
        )

    def summed(parts):
        return call(sum_kernel, parts, [low_block(top_rows)])[0]

    steps = [1 << n for n in range(dp_size.bit_length() - 1)]
    (rest,) = rest_call(0, [mixed_grad])
    total = summed([after(piece, rest) for piece in top_got])
    layer_got = exchange([after(piece, total) for piece in layer_pieces])
    beside_calls = steps[: groups - 1]
    for s in range(1, groups):
        coming = hop_dp(total, beside_calls[s - 1]) if s <= len(beside_calls) else None
        if s < groups - 1:
            held = after(mixed_grad, total)
            (rest,) = rest_call(s, [held, rest])
            mark = rest
        else:
            held = after(mixed_grad, total, layer_got[1])
            embed_pieces = rest_call(s, [held, rest, back_middle, x, gain_first, top_grad])
            mark = embed_pieces[0]
        if s == groups - 1:
            break
        if coming is not None:
            total = summed([after(total, mark), after(coming, mark)])
    for distance in steps[groups - 1 :]:
        total = summed([total, coming])
        coming = hop_dp(total, distance)
    half = shard_rows // 2
    leaving = [shard_rows + top_rows] * 2 + [half, half]
    total, *leaving_pieces = call(
        append_kernel,
        [after(total, mark), after(coming, mark), *embed_pieces[1:]],
        [low_block(top_rows)] + [low_block(count) for count in leaving],
    )
    near, across, top_half, low_half = (
        hop(after(piece, *layer_got[1:]), d) for piece, d in zip(leaving_pieces, (1, 2, 3, 3))
    )

    (passed,) = call(
        functools.partial(split_kernel, (shard_rows,)), [across], [low_block(top_rows)]
    )
    diagonal = hop(passed, 1)

    def embed_call(start, blocks, starts, earlier):
        return call(
            functools.partial(embed_kernel, (start, half, starts)),
            [*blocks, *earlier],
            [((shard_rows, groups, width), F32)],
            [
                ((groups, half, width), BF16),
                ((half, groups, width), F32),
                dma((2,)),
            ],
            out_space=None,
            far_outs=1,
            far_last=len(earlier),
        )[0]

    embed_grad = embed_call(0, [embed_pieces[0], near, across, top_half], (0, 0, 0, 0), [])
    grad_block, new_left, new_right, new_prompt = call(
        functools.partial(step_kernel, (prompt_rows, groups, (0, shard_rows, shard_rows, 0))),
        [after(total, embed_grad), near, across, diagonal, left_stat, right_stat, left_root, right_root, prompt.T],
        [
            ((prompt_rows // groups, width), F32),
            (left_stat.shape, F32),
            (right_stat.shape, F32),
            ((prompt_cols, prompt_rows), F32),
        ],
        [low_block(TILE)],
        out_space=None,
    )
    low_half = after(low_half, grad_block)
    embed_grad = embed_call(
        half, [embed_pieces[0], near, across, low_half], (half, half, half, 0), [embed_grad]
    )

    def merged(got, kind):
        return call(
            merge_kernel,
            got,
            [((shard_rows, groups, width), kind)],
            [((groups, shard_rows, width), BF16)],
            out_space=None,
        )[0]

    layer_out = merged(layer_got, BF16)
    return (layer_out, embed_grad, grad_block, new_left, new_right, new_prompt.T)


def solution(mesh):
    placed = (
        P("mp", "dp", None),
        P("mp", "dp", None),
        P("dp"),
        P(None, "dp"),
        P(),
        P(),
        P(None, "mp"),
        P(None, "mp"),
        P(None, "mp"),
        P("mp", None),
        P(None, "mp"),
        P("mp", None),
        P(None, "mp"),
        P(),
        P("dp", None),
        P(),
        P("dp", None),
    )
    return jax.shard_map(
        on_device,
        mesh=mesh,
        in_specs=placed,
        out_specs=(
            P("mp", "dp", None),
            P("mp", "dp", None),
            P("mp", None),
            P(),
            P("dp", None),
            P(None, "dp"),
        ),
        check_vma=False,
    )
```
